256 devices in a mesh: rep: 8 (over x, core), row: 8 (over z), col: 4 (over y).
Axes of the slice: x: 4, y: 4, z: 8, core: 2. Of those that a mesh axis runs over, the one named last changes fastest.
Arguments:
- grad_parts: bfloat16 [8, 2, 8, 512, 14336], P('rep', None, None, 'row', 'col'), may hold values from -100 to 100, as said below
- weights: float32 [2, 4096, 14336], P(None, ('rep', 'row'), 'col'), may hold values from -1.5 to 1.5
Outputs:
- updated: float32 [2, 4096, 14336], P(None, ('rep', 'row'), 'col')
- direction: float32 [2, 4096, 14336], P(None, ('rep', 'row'), 'col')
The draws below stay inside these ranges and needn't reach their ends.
Inputs may be any that keep to these rules, and one draw needn't show every extreme that they name: `grad_parts`: finite partial gradients.
All inputs are finite; a program needn't handle non-finite values.
Results may differ from the reference program's by a relative error of at most 0.0003.
Values sent between devices are 32-bit elements; how exact they have to be, the bound alone decides.
No kernel may reach another device: no remote copies, remote signals or barrier semaphores. Data moves between devices by JAX's collectives and lax.ppermute only.
A program may use at most 128 MiB of HBM per device.

```python
import math
import jax
import jax.numpy as jnp
from jax import lax

DW = 4096
FW = 14336
ITERS = 5
BLOCKS = 8


def draw_grad_parts(key, part):
    keys = jax.random.split(key, 8)
    rising = 1.7320508
    row_index = jnp.arange(DW, dtype=jnp.float32)
    col_index = jnp.arange(FW, dtype=jnp.float32)
    row_scale = jnp.exp(jax.random.uniform(keys[0], (2, DW), jnp.float32, 0.0, math.log(10.0))) * rising ** (row_index / DW)
    col_scale = jnp.exp(jax.random.uniform(keys[1], (2, FW), jnp.float32, 0.0, math.log(10.0))) * rising ** (col_index / FW)
    row_rank = jnp.stack([jax.random.permutation(keys[4], DW), jax.random.permutation(keys[5], DW)]).astype(jnp.float32)
    col_rank = jnp.stack([jax.random.permutation(keys[6], FW), jax.random.permutation(keys[7], FW)]).astype(jnp.float32)
    row_place = ((row_rank + 0.5) / DW) ** 2
    col_place = (col_rank + 0.5) / FW
    profile = 0.05 + jnp.exp(-jnp.abs(row_place[:, :, None] - col_place[:, None, :]) / 0.05)
    noise = jax.random.normal(keys[2], (BLOCKS, 2, DW, FW), jnp.float32)
    block_of_row = jnp.floor(row_index / (DW // BLOCKS))
    replica = jnp.arange(BLOCKS, dtype=jnp.float32)
    spike = 1.0 + 2.0 * (block_of_row[None, None, :, None] == replica[:, None, None, None]).astype(jnp.float32)
    values = 0.02 * noise * spike * row_scale[None, :, :, None] * col_scale[None, :, None, :] * profile[None]
    values = jnp.clip(values, -100.0, 100.0)
    return values.reshape(BLOCKS, 2, BLOCKS, DW // BLOCKS, FW).astype(jnp.bfloat16)


def steps_of(rng, dims, cuts, low, top_value):
    def one(position, shards_of):
        heights = jax.random.uniform(jax.random.fold_in(jax.random.fold_in(rng, 6), position), (shards_of,), jnp.float32, low / len(cuts), top_value / len(cuts))
        return jnp.repeat(jnp.exp(heights), dims[position] // shards_of).reshape((-1,) + (1,) * (len(dims) - position - 1))

    level = one(*cuts[0])
    for cut in cuts[1:]:
        level = level * one(*cut)
    return level


def gaussian(rng, shape, spread, most, shards=(), kind=jnp.bfloat16):
    drawn = spread * jax.random.normal(rng, shape, jnp.float32)
    if shards:
        drawn = drawn * steps_of(rng, shape, shards, -0.22, 0.18)
    return jnp.clip(drawn, -most, most).astype(kind)


def setup_inputs(seed: int = 0) -> dict:
    key_of = jax.random.split(jax.random.key(seed), 3)
    return {
        "grad_parts": draw_grad_parts(jax.random.fold_in(key_of[2], 71), 0),
        "weights": gaussian(key_of[1], (2, DW, FW), 0.25, 1.5, ((1, 64), (2, 4)), jnp.float32),
    }


EPSILON = 1e-06
LEARNING_RATE = 0.02
DECAY_RATE = 0.1

def reference(grad_parts, weights):

    def accumulate(carry, part):
        return (carry + part.astype(jnp.float32), None)
    start = jnp.zeros(grad_parts.shape[1:], jnp.float32)
    summed, unused = lax.scan(accumulate, start, grad_parts)
    direction = summed.reshape(2, DW, FW)
    for sweep in range(ITERS):
        row_total = lax.optimization_barrier(jnp.sum(direction * direction, axis=2, keepdims=True))
        direction = direction * lax.rsqrt(row_total / FW + EPSILON)
        column_total = lax.optimization_barrier(jnp.sum(direction * direction, axis=1, keepdims=True))
        direction = direction * lax.rsqrt(column_total / DW + EPSILON)
    updated = weights * (1.0 - LEARNING_RATE * DECAY_RATE) - LEARNING_RATE * direction
    return (updated, direction)
```

```python
import jax
import jax.numpy as jnp
from jax import lax
from jax.experimental import pallas as pl
from jax.experimental.pallas import tpu as pltpu
from jax.sharding import Mesh
from jax.sharding import PartitionSpec as P

DW = 4096
FW = 14336
ITERS = 5


EPSILON = 1e-06
LEARNING_RATE = 0.02
DECAY_RATE = 0.1


def widen_kernel(place, grads, first, second):
    first[0] = grads[0, 0, 0].astype(jnp.float32)
    second[0] = grads[1, 0, 0].astype(jnp.float32)


def widen_add_kernel(place, grads, other_first, other_second, first, second):
    first[0] = grads[0, 0, 0].astype(jnp.float32) + other_first[0]
    second[0] = grads[1, 0, 0].astype(jnp.float32) + other_second[0]


def widen(grads, place, others=()):
    _, groups, _, rows, columns = grads.shape
    width = columns // groups
    flat = pl.BlockSpec((1, rows, width), lambda j, place: (j, 0, 0))
    return pl.pallas_call(
        widen_add_kernel if others else widen_kernel,
        grid_spec=pltpu.PrefetchScalarGridSpec(
            num_scalar_prefetch=1,
            grid=(groups,),
            in_specs=[
                pl.BlockSpec(
                    (2, 1, 1, rows, width), lambda j, place: (0, j, place[0], 0, place[1])
                )
            ]
            + [flat] * len(others),
            out_specs=[flat, flat],
        ),
        out_shape=[jax.ShapeDtypeStruct((groups, rows, width), jnp.float32)] * 2,
    )(place, grads, *others)


def reduce_scatter(grads, size):
    x = lax.axis_index("x")
    core = lax.axis_index("core")

    def place(which, step):
        return jnp.stack([which, lax.rem(x + step, size)]).astype(jnp.int32)

    def move(values, step):
        return lax.ppermute(values, "x", [(i, (i + step) % size) for i in range(size)])

    total = {}
    for step in (2, 1, 3, 0):
        sent = widen(grads, place(1 - core, step))
        other = [lax.ppermute(s, "core", [(0, 1), (1, 0)]) for s in sent]
        total[step] = widen(grads, place(core, step), other)
    right = move(total[2][0], 1)
    left = move(total[2][1], -1)
    right_plain = move(total[1][1], 1)
    left_plain = move(total[3][0], -1)
    right_summed = move(total[1][0] + right, 1)
    left_summed = move(total[3][1] + left, -1)
    return (
        total[0][0] + left_plain + right_summed,
        total[0][1] + right_plain + left_summed,
    )


def group_sum(parts, axes, size):
    flat = jnp.concatenate(parts)[None, :]
    spread = jnp.broadcast_to(flat[None], (size,) + flat.shape)
    total = jnp.sum(lax.all_to_all(spread, axes, 0, 0, tiled=True), axis=(0, 1))
    return jnp.split(total, 2)


def per_device(sizes, grad_parts, weights):
    size_x, size_core, size_row, size_col = sizes
    _, _, blocks, rows, columns = grad_parts.shape
    grads = grad_parts.reshape(2, size_x, size_core, rows, columns)
    summed = reduce_scatter(grads, size_x)
    width = columns // size_x
    values = [s.reshape(size_x * rows, width) for s in summed]
    for sweep in range(ITERS):
        totals = group_sum(
            [jnp.sum(v * v, axis=1) for v in values], ("x", "col"), size_x * size_col
        )
        values = [v * lax.rsqrt(t / FW + EPSILON)[:, None] for v, t in zip(values, totals)]
        totals = group_sum(
            [jnp.sum(v * v, axis=0) for v in values], ("core", "row"), size_core * size_row
        )
        values = [v * lax.rsqrt(t / DW + EPSILON)[None, :] for v, t in zip(values, totals)]
    direction = jnp.stack([v.reshape(size_x, rows, width) for v in values], axis=1)
    direction = lax.all_to_all(direction, "x", 0, 0, tiled=True)
    direction = direction.transpose(1, 2, 0, 3).reshape(2, rows, columns)
    updated = weights * (1.0 - LEARNING_RATE * DECAY_RATE) - LEARNING_RATE * direction
    return (updated, direction)


def solution(mesh):
    size_core = 2
    size_x = mesh.shape["rep"] // size_core
    sizes = (size_x, size_core, mesh.shape["row"], mesh.shape["col"])
    split = Mesh(mesh.devices.reshape(sizes), ("x", "core", "row", "col"))
    rep = ("x", "core")
    in_specs = (P(rep, None, None, "row", "col"), P(None, rep + ("row",), "col"))
    out_specs = (P(None, rep + ("row",), "col"), P(None, rep + ("row",), "col"))

    def run(grad_parts, weights):
        return per_device(sizes, grad_parts, weights)

    return jax.shard_map(
        run, mesh=split, in_specs=in_specs, out_specs=out_specs, check_vma=False
    )
```

```python
import functools

import jax
import jax.numpy as jnp
from jax import lax
from jax.experimental import pallas as pl
from jax.experimental.pallas import tpu as pltpu
from jax.sharding import Mesh
from jax.sharding import PartitionSpec as P

DW = 4096
FW = 14336
ITERS = 5


EPSILON = 1e-06
LEARNING_RATE = 0.02
DECAY_RATE = 0.1
CORES = 2


def widen_kernel(steps, own, place, *refs):
    grads = refs[:steps]
    if own:
        other, outs = refs[steps], refs[steps + 1 :]
        for out in range(2 * steps):
            step, half = divmod(out, 2)
            outs[out][...] = grads[step][0, :, half].astype(jnp.float32) + other[step, half]
    else:
        for step in range(steps):
            for half in range(2):
                refs[-1][step, half] = grads[step][0, :, half].astype(jnp.float32)


def widen(grads, place, size, steps, other=None):
    _, groups, _, rows, columns = grads.shape
    width = columns // size
    deep = groups // 2
    own = other is not None

    def source(step):
        def index(j, place):
            matrix = place[1] if own else 1 - place[1]
            return (matrix, j, 0, 0, lax.rem(place[0] + step, size))

        return pl.BlockSpec((1, deep, 2, rows, width), index)

    flat = pl.BlockSpec((deep, rows, width), lambda j, place: (j, 0, 0))
    count = len(steps)
    joined = pl.BlockSpec((count, 2, deep, rows, width), lambda j, place: (0, 0, j, 0, 0))
    shape = (groups, rows, width)
    shapes = [shape] * (2 * count) if own else [(count, 2) + shape]
    return pl.pallas_call(
        functools.partial(widen_kernel, count, own),
        grid_spec=pltpu.PrefetchScalarGridSpec(
            num_scalar_prefetch=1,
            grid=(2,),
            in_specs=[source(step) for step in steps] + ([joined] if own else []),
            out_specs=[flat] * (2 * count) if own else [joined],
        ),
        out_shape=[jax.ShapeDtypeStruct(s, jnp.float32) for s in shapes],
        compiler_params=pltpu.CompilerParams(vmem_limit_bytes=40 * 2**20),
    )(place, *[grads] * count, *([other] if own else []))


def swap(values):
    return lax.ppermute(values, "core", [(0, 1), (1, 0)])


def move(values, size, step):
    return lax.ppermute(values, "x", [(i, (i + step) % size) for i in range(size)])


def after(values, earlier):
    return lax.optimization_barrier((values, earlier))[0]


def reduce_scatter(grads, place, size):
    def total(steps, place):
        other = swap(widen(grads, place, size, steps)[0])
        return widen(grads, place, size, steps, other)

    far_first, far_second = total((2,), place)
    right = move(far_first, size, 1)
    left = move(far_second, size, -1)
    next_first, next_second, last_first, last_second = total((1, 3), after(place, far_first))
    right_plain = move(next_second, size, 1)
    left_plain = move(last_first, size, -1)
    first, second = total((0,), after(place, far_first))
    next_first, last_second, right, left, first, second = lax.optimization_barrier(
        (next_first, last_second, right, left, first, second)
    )
    right_summed = move(next_first + right, size, 1)
    left_summed = move(last_second + left, size, -1)
    first = first + left_plain
    second = second + right_plain
    return first + right_summed, second + left_summed


def group_sum(part, axes, size):
    spread = jnp.broadcast_to(part[None, None, :], (size, 1) + part.shape)
    return jnp.sum(lax.all_to_all(spread, axes, 0, 0, tiled=True), axis=(0, 1))


def per_device(sizes, grad_parts, weights):
    size_x, size_row, size_col = sizes
    _, _, blocks, rows, columns = grad_parts.shape
    x = lax.axis_index("x")
    core = lax.axis_index("core")
    place = jnp.stack([x, core]).astype(jnp.int32)
    grads = grad_parts.reshape(2, size_x, CORES, rows, columns)
    halves = reduce_scatter(grads, place, size_x)
    width = columns // size_x

    values = [h.reshape(size_x * rows, width) for h in halves]
    row_factor = jnp.ones((CORES, size_x * rows), jnp.float32)
    column_factor = jnp.ones((width,), jnp.float32)

    def scaled():
        return [
            v * r[:, None] * column_factor[None, :] for v, r in zip(values, row_factor)
        ]

    for sweep in range(ITERS):
        part = jnp.concatenate([jnp.sum(v * v, axis=1) for v in scaled()])
        total = group_sum(part, ("x", "col"), size_x * size_col)
        row_factor = row_factor * lax.rsqrt(total / FW + EPSILON).reshape(CORES, -1)
        part = sum(jnp.sum(v * v, axis=0) for v in scaled())
        total = group_sum(part, ("row",), size_row)
        column_factor = column_factor * lax.rsqrt(total / DW + EPSILON)

    direction = jnp.stack([v.reshape(size_x, rows, width) for v in scaled()], axis=1)
    direction = direction.reshape(blocks, rows, width)
    direction = lax.all_to_all(direction, ("x", "core"), 0, 0, tiled=True)
    direction = direction.reshape(size_x, CORES, rows, width).transpose(1, 2, 0, 3)
    direction = direction.reshape(CORES, rows, columns)
    updated = weights * (1.0 - LEARNING_RATE * DECAY_RATE) - LEARNING_RATE * direction
    return (updated, direction)


def solution(mesh):
    size_x = mesh.shape["rep"] // CORES
    sizes = (size_x, mesh.shape["row"], mesh.shape["col"])
    split = Mesh(
        mesh.devices.reshape((size_x, CORES) + sizes[1:]), ("x", "core", "row", "col")
    )
    rep = ("x", "core")
    in_specs = (P(rep, None, None, "row", "col"), P(None, rep + ("row",), "col"))
    out_specs = (P(None, rep + ("row",), "col"), P(None, rep + ("row",), "col"))

    def run(grad_parts, weights):
        return per_device(sizes, grad_parts, weights)

    return jax.shard_map(
        run, mesh=split, in_specs=in_specs, out_specs=out_specs, check_vma=False
    )
```

```python
import functools

import jax
import jax.numpy as jnp
from jax import lax
from jax.experimental import pallas as pl
from jax.experimental.pallas import tpu as pltpu
from jax.sharding import Mesh
from jax.sharding import PartitionSpec as P

DW = 4096
FW = 14336
ITERS = 5


EPSILON = 1e-06
LEARNING_RATE = 0.02
DECAY_RATE = 0.1
CORES = 2


def widen_kernel(steps, own, place, *refs):
    grads = refs[:steps]
    if own:
        other, outs = refs[steps], refs[steps + 1 :]
        for out in range(2 * steps):
            step, half = divmod(out, 2)
            outs[out][...] = grads[step][0, :, half].astype(jnp.float32) + other[step, half]
    else:
        for step in range(steps):
            for half in range(2):
                refs[-1][step, half] = grads[step][0, :, half].astype(jnp.float32)


def widen(grads, place, size, steps, other=None):
    _, groups, _, rows, columns = grads.shape
    width = columns // size
    deep = groups // 2
    own = other is not None

    def source(step):
        def index(j, place):
            matrix = place[1] if own else 1 - place[1]
            return (matrix, j, 0, 0, lax.rem(place[0] + step, size))

        return pl.BlockSpec((1, deep, 2, rows, width), index)

    flat = pl.BlockSpec((deep, rows, width), lambda j, place: (j, 0, 0))
    count = len(steps)
    joined = pl.BlockSpec((count, 2, deep, rows, width), lambda j, place: (0, 0, j, 0, 0))
    shape = (groups, rows, width)
    shapes = [shape] * (2 * count) if own else [(count, 2) + shape]
    return pl.pallas_call(
        functools.partial(widen_kernel, count, own),
        grid_spec=pltpu.PrefetchScalarGridSpec(
            num_scalar_prefetch=1,
            grid=(2,),
            in_specs=[source(step) for step in steps] + ([joined] if own else []),
            out_specs=[flat] * (2 * count) if own else [joined],
        ),
        out_shape=[jax.ShapeDtypeStruct(s, jnp.float32) for s in shapes],
        compiler_params=pltpu.CompilerParams(vmem_limit_bytes=40 * 2**20),
    )(place, *[grads] * count, *([other] if own else []))


def swap(values):
    return lax.ppermute(values, "core", [(0, 1), (1, 0)])


def move(values, size, step):
    return lax.ppermute(values, "x", [(i, (i + step) % size) for i in range(size)])


def after(values, earlier):
    return lax.optimization_barrier((values, earlier))[0]


def reduce_scatter(grads, place, size):
    def total(steps, place):
        other = swap(widen(grads, place, size, steps)[0])
        return widen(grads, place, size, steps, other)

    far_first, far_second = total((2,), place)
    right = move(far_first, size, 1)
    left = move(far_second, size, -1)
    parts = total((1, 3, 0), after(place, far_first))
    next_first, next_second, last_first, last_second, first, second = parts
    right_plain = move(next_second, size, 1)
    left_plain = move(last_first, size, -1)
    right_summed = move(next_first + right, size, 1)
    left_summed = move(last_second + left, size, -1)
    first = first + left_plain
    second = second + right_plain
    return first + right_summed, second + left_summed


def group_sum(part, axes, size):
    spread = jnp.broadcast_to(part[None, None, :], (size, 1) + part.shape)
    return jnp.sum(lax.all_to_all(spread, axes, 0, 0, tiled=True), axis=(0, 1))


def update_kernel(pieces, weights, updated, direction):
    values = pieces[...]
    direction[...] = values
    updated[...] = weights[...] * (1.0 - LEARNING_RATE * DECAY_RATE) - LEARNING_RATE * values


def update(pieces, weights):
    _, rows, width = pieces.shape
    side = pl.BlockSpec((CORES, rows, width), lambda i: (0, 0, i))
    return pl.pallas_call(
        update_kernel,
        grid=(pieces.shape[0] // CORES,),
        in_specs=[pl.BlockSpec((CORES, rows, width), lambda i: (i, 0, 0)), side],
        out_specs=[side, side],
        out_shape=[jax.ShapeDtypeStruct(weights.shape, jnp.float32)] * 2,
        compiler_params=pltpu.CompilerParams(vmem_limit_bytes=40 * 2**20),
    )(pieces, weights)


def per_device(sizes, grad_parts, weights):
    size_x, size_row, size_col = sizes
    _, _, blocks, rows, columns = grad_parts.shape
    x = lax.axis_index("x")
    core = lax.axis_index("core")
    place = jnp.stack([x, core]).astype(jnp.int32)
    grads = grad_parts.reshape(2, size_x, CORES, rows, columns)
    halves = reduce_scatter(grads, place, size_x)
    width = columns // size_x

    values = [h.reshape(size_x * rows, width) for h in halves]
    row_factor = jnp.ones((CORES, size_x * rows), jnp.float32)
    column_factor = jnp.ones((width,), jnp.float32)

    def scaled():
        return [
            v * r[:, None] * column_factor[None, :] for v, r in zip(values, row_factor)
        ]

    for sweep in range(ITERS):
        part = jnp.concatenate([jnp.sum(v * v, axis=1) for v in scaled()])
        total = group_sum(part, ("x", "col"), size_x * size_col)
        row_factor = row_factor * lax.rsqrt(total / FW + EPSILON).reshape(CORES, -1)
        part = sum(jnp.sum(v * v, axis=0) for v in scaled())
        total = group_sum(part, ("row",), size_row)
        column_factor = column_factor * lax.rsqrt(total / DW + EPSILON)

    direction = jnp.stack([v.reshape(size_x, rows, width) for v in scaled()], axis=1)
    direction = direction.reshape(blocks, rows, width)
    direction = lax.all_to_all(direction, ("x", "core"), 0, 0, tiled=True)
    return update(direction, weights)


def solution(mesh):
    size_x = mesh.shape["rep"] // CORES
    sizes = (size_x, mesh.shape["row"], mesh.shape["col"])
    split = Mesh(
        mesh.devices.reshape((size_x, CORES) + sizes[1:]), ("x", "core", "row", "col")
    )
    rep = ("x", "core")
    in_specs = (P(rep, None, None, "row", "col"), P(None, rep + ("row",), "col"))
    out_specs = (P(None, rep + ("row",), "col"), P(None, rep + ("row",), "col"))

    def run(grad_parts, weights):
        return per_device(sizes, grad_parts, weights)

    return jax.shard_map(
        run, mesh=split, in_specs=in_specs, out_specs=out_specs, check_vma=False
    )
```

```python
import functools

import jax
import jax.numpy as jnp
from jax import lax
from jax.experimental import pallas as pl
from jax.experimental.pallas import tpu as pltpu
from jax.sharding import Mesh
from jax.sharding import PartitionSpec as P

DW = 4096
FW = 14336
ITERS = 5


EPSILON = 1e-06
LEARNING_RATE = 0.02
DECAY_RATE = 0.1
CORES = 2


def widen_kernel(steps, own, place, *refs):
    grads = refs[:steps]
    if own:
        other, outs = refs[steps], refs[steps + 1 :]
        for out in range(2 * steps):
            step, half = divmod(out, 2)
            outs[out][...] = grads[step][0, :, half].astype(jnp.float32) + other[step, half]
    else:
        for step in range(steps):
            for half in range(2):
                refs[-1][step, half] = grads[step][0, :, half].astype(jnp.float32)


def widen(grads, place, size, steps, other=None):
    _, groups, _, rows, columns = grads.shape
    width = columns // size
    deep = groups // 2
    own = other is not None

    def source(step):
        def index(j, place):
            matrix = place[1] if own else 1 - place[1]
            return (matrix, j, 0, 0, lax.rem(place[0] + step, size))

        return pl.BlockSpec((1, deep, 2, rows, width), index)

    flat = pl.BlockSpec((deep, rows, width), lambda j, place: (j, 0, 0))
    count = len(steps)
    joined = pl.BlockSpec((count, 2, deep, rows, width), lambda j, place: (0, 0, j, 0, 0))
    shape = (groups, rows, width)
    shapes = [shape] * (2 * count) if own else [(count, 2) + shape]
    return pl.pallas_call(
        functools.partial(widen_kernel, count, own),
        grid_spec=pltpu.PrefetchScalarGridSpec(
            num_scalar_prefetch=1,
            grid=(2,),
            in_specs=[source(step) for step in steps] + ([joined] if own else []),
            out_specs=[flat] * (2 * count) if own else [joined],
        ),
        out_shape=[jax.ShapeDtypeStruct(s, jnp.float32) for s in shapes],
        compiler_params=pltpu.CompilerParams(vmem_limit_bytes=40 * 2**20),
    )(place, *[grads] * count, *([other] if own else []))


def swap(values):
    return lax.ppermute(values, "core", [(0, 1), (1, 0)])


def move(values, size, step):
    return lax.ppermute(values, "x", [(i, (i + step) % size) for i in range(size)])


def after(values, earlier):
    return lax.optimization_barrier((values, earlier))[0]


def reduce_scatter(grads, place, size):
    def total(steps, place):
        other = swap(widen(grads, place, size, steps)[0])
        return widen(grads, place, size, steps, other)

    far_first, far_second = total((2,), place)
    right = move(far_first, size, 1)
    left = move(far_second, size, -1)
    parts = total((1, 3, 0), after(place, far_first))
    next_first, next_second, last_first, last_second, first, second = parts
    right_plain = move(next_second, size, 1)
    left_plain = move(last_first, size, -1)
    right_summed = move(next_first + right, size, 1)
    left_summed = move(last_second + left, size, -1)
    first = first + left_plain
    second = second + right_plain
    return first + right_summed, second + left_summed


def group_sum(part, axes, size):
    spread = jnp.broadcast_to(part[None, None, :], (size, 1) + part.shape)
    return jnp.sum(lax.all_to_all(spread, axes, 0, 0, tiled=True), axis=(0, 1))


def update_kernel(pieces, weights, updated, direction):
    values = pieces[...]
    direction[...] = values
    updated[...] = weights[...] * (1.0 - LEARNING_RATE * DECAY_RATE) - LEARNING_RATE * values


def update(pieces, weights):
    _, rows, width = pieces.shape
    side = pl.BlockSpec((CORES, rows, width), lambda i: (0, 0, i))
    return pl.pallas_call(
        update_kernel,
        grid=(pieces.shape[0] // CORES,),
        in_specs=[pl.BlockSpec((CORES, rows, width), lambda i: (i, 0, 0)), side],
        out_specs=[side, side],
        out_shape=[jax.ShapeDtypeStruct(weights.shape, jnp.float32)] * 2,
        compiler_params=pltpu.CompilerParams(vmem_limit_bytes=40 * 2**20),
    )(pieces, weights)


def per_device(sizes, grad_parts, weights):
    size_x, size_row, size_col = sizes
    _, _, blocks, rows, columns = grad_parts.shape
    x = lax.axis_index("x")
    core = lax.axis_index("core")
    place = jnp.stack([x, core]).astype(jnp.int32)
    grads = grad_parts.reshape(2, size_x, CORES, rows, columns)
    halves = reduce_scatter(grads, place, size_x)
    width = columns // size_x

    halves = lax.optimization_barrier(halves)
    values = [jnp.concatenate(halves).reshape(blocks * rows, width)]
    row_factor = jnp.ones((1, blocks * rows), jnp.float32)
    column_factor = jnp.ones((width,), jnp.float32)

    def scaled():
        return [
            v * r[:, None] * column_factor[None, :] for v, r in zip(values, row_factor)
        ]

    for sweep in range(ITERS):
        part = jnp.concatenate([jnp.sum(v * v, axis=1) for v in scaled()])
        total = group_sum(part, ("x", "col"), size_x * size_col)
        row_factor = row_factor * lax.rsqrt(total / FW + EPSILON).reshape(1, -1)
        part = sum(jnp.sum(v * v, axis=0) for v in scaled())
        total = group_sum(part, ("row",), size_row)
        column_factor = column_factor * lax.rsqrt(total / DW + EPSILON)

    direction = scaled()[0].reshape(CORES, size_x, rows, width).transpose(1, 0, 2, 3)
    direction = direction.reshape(blocks, rows, width)
    direction = lax.all_to_all(direction, ("x", "core"), 0, 0, tiled=True)
    return update(direction, weights)


def solution(mesh):
    size_x = mesh.shape["rep"] // CORES
    sizes = (size_x, mesh.shape["row"], mesh.shape["col"])
    split = Mesh(
        mesh.devices.reshape((size_x, CORES) + sizes[1:]), ("x", "core", "row", "col")
    )
    rep = ("x", "core")
    in_specs = (P(rep, None, None, "row", "col"), P(None, rep + ("row",), "col"))
    out_specs = (P(None, rep + ("row",), "col"), P(None, rep + ("row",), "col"))

    def run(grad_parts, weights):
        return per_device(sizes, grad_parts, weights)

    return jax.shard_map(
        run, mesh=split, in_specs=in_specs, out_specs=out_specs, check_vma=False
    )
```

```python
import functools

import jax
import jax.numpy as jnp
from jax import lax
from jax.experimental import pallas as pl
from jax.experimental.pallas import tpu as pltpu
from jax.sharding import Mesh
from jax.sharding import PartitionSpec as P

DW = 4096
FW = 14336
ITERS = 5


EPSILON = 1e-06
LEARNING_RATE = 0.02
DECAY_RATE = 0.1
CORES = 2


def widen_kernel(steps, own, place, *refs):
    grads = refs[:steps]
    if own:
        other, outs = refs[steps], refs[steps + 1 :]
        for out in range(2 * steps):
            step, half = divmod(out, 2)
            outs[out][...] = grads[step][0, :, half].astype(jnp.float32) + other[step, half]
    else:
        for step in range(steps):
            for half in range(2):
                refs[-1][step, half] = grads[step][0, :, half].astype(jnp.float32)


def widen(grads, place, size, steps, other=None):
    _, groups, _, rows, columns = grads.shape
    width = columns // size
    deep = groups // 2
    own = other is not None

    def source(step):
        def index(j, place):
            matrix = place[1] if own else 1 - place[1]
            return (matrix, j, 0, 0, lax.rem(place[0] + step, size))

        return pl.BlockSpec((1, deep, 2, rows, width), index)

    flat = pl.BlockSpec((deep, rows, width), lambda j, place: (j, 0, 0))
    count = len(steps)
    joined = pl.BlockSpec((count, 2, deep, rows, width), lambda j, place: (0, 0, j, 0, 0))
    shape = (groups, rows, width)
    shapes = [shape] * (2 * count) if own else [(count, 2) + shape]
    return pl.pallas_call(
        functools.partial(widen_kernel, count, own),
        grid_spec=pltpu.PrefetchScalarGridSpec(
            num_scalar_prefetch=1,
            grid=(2,),
            in_specs=[source(step) for step in steps] + ([joined] if own else []),
            out_specs=[flat] * (2 * count) if own else [joined],
        ),
        out_shape=[jax.ShapeDtypeStruct(s, jnp.float32) for s in shapes],
        compiler_params=pltpu.CompilerParams(vmem_limit_bytes=40 * 2**20),
    )(place, *[grads] * count, *([other] if own else []))


def swap(values):
    return lax.ppermute(values, "core", [(0, 1), (1, 0)])


def move(values, size, step):
    return lax.ppermute(values, "x", [(i, (i + step) % size) for i in range(size)])


def after(values, earlier):
    return lax.optimization_barrier((values, earlier))[0]


def reduce_scatter(grads, place, size):
    def total(steps, sent):
        return widen(grads, place, size, steps, swap(sent))

    (sent,) = widen(grads, place, size, (2,))
    (sent_later,) = widen(grads, after(place, sent), size, (1, 3, 0))
    far_first, far_second = total((2,), sent)
    right = move(far_first, size, 1)
    left = move(far_second, size, -1)
    parts = total((1, 3, 0), after(sent_later, far_first))
    next_first, next_second, last_first, last_second, first, second = parts
    right_plain = move(next_second, size, 1)
    left_plain = move(last_first, size, -1)
    right_summed = move(next_first + right, size, 1)
    left_summed = move(last_second + left, size, -1)
    first = first + left_plain
    second = second + right_plain
    return first + right_summed, second + left_summed


def group_sum(part, axes, size):
    spread = jnp.broadcast_to(part[None, None, :], (size, 1) + part.shape)
    return jnp.sum(lax.all_to_all(spread, axes, 0, 0, tiled=True), axis=(0, 1))


def update_kernel(pieces, weights, updated, direction):
    values = pieces[...]
    direction[...] = values
    updated[...] = weights[...] * (1.0 - LEARNING_RATE * DECAY_RATE) - LEARNING_RATE * values


def update(pieces, weights):
    _, rows, width = pieces.shape
    side = pl.BlockSpec((CORES, rows, width), lambda i: (0, 0, i))
    return pl.pallas_call(
        update_kernel,
        grid=(pieces.shape[0] // CORES,),
        in_specs=[pl.BlockSpec((CORES, rows, width), lambda i: (i, 0, 0)), side],
        out_specs=[side, side],
        out_shape=[jax.ShapeDtypeStruct(weights.shape, jnp.float32)] * 2,
        compiler_params=pltpu.CompilerParams(vmem_limit_bytes=40 * 2**20),
    )(pieces, weights)


def per_device(sizes, grad_parts, weights):
    size_x, size_row, size_col = sizes
    _, _, blocks, rows, columns = grad_parts.shape
    x = lax.axis_index("x")
    core = lax.axis_index("core")
    place = jnp.stack([x, core]).astype(jnp.int32)
    grads = grad_parts.reshape(2, size_x, CORES, rows, columns)
    halves = reduce_scatter(grads, place, size_x)
    width = columns // size_x

    halves = lax.optimization_barrier(halves)
    values = [jnp.concatenate(halves).reshape(blocks * rows, width)]
    row_factor = jnp.ones((1, blocks * rows), jnp.float32)
    column_factor = jnp.ones((width,), jnp.float32)

    def scaled():
        return [
            v * r[:, None] * column_factor[None, :] for v, r in zip(values, row_factor)
        ]

    for sweep in range(ITERS):
        part = jnp.concatenate([jnp.sum(v * v, axis=1) for v in scaled()])
        total = group_sum(part, ("x", "col"), size_x * size_col)
        row_factor = row_factor * lax.rsqrt(total / FW + EPSILON).reshape(1, -1)
        part = sum(jnp.sum(v * v, axis=0) for v in scaled())
        total = group_sum(part, ("row",), size_row)
        column_factor = column_factor * lax.rsqrt(total / DW + EPSILON)

    direction = scaled()[0].reshape(CORES, size_x, rows, width).transpose(1, 0, 2, 3)
    direction = direction.reshape(blocks, rows, width)
    direction = lax.all_to_all(direction, ("x", "core"), 0, 0, tiled=True)
    return update(direction, weights)


def solution(mesh):
    size_x = mesh.shape["rep"] // CORES
    sizes = (size_x, mesh.shape["row"], mesh.shape["col"])
    split = Mesh(
        mesh.devices.reshape((size_x, CORES) + sizes[1:]), ("x", "core", "row", "col")
    )
    rep = ("x", "core")
    in_specs = (P(rep, None, None, "row", "col"), P(None, rep + ("row",), "col"))
    out_specs = (P(None, rep + ("row",), "col"), P(None, rep + ("row",), "col"))

    def run(grad_parts, weights):
        return per_device(sizes, grad_parts, weights)

    return jax.shard_map(
        run, mesh=split, in_specs=in_specs, out_specs=out_specs, check_vma=False
    )
```

```python
import functools

import jax
import jax.numpy as jnp
from jax import lax
from jax.experimental import pallas as pl
from jax.experimental.pallas import tpu as pltpu
from jax.sharding import Mesh
from jax.sharding import PartitionSpec as P

DW = 4096
FW = 14336
ITERS = 5


EPSILON = 1e-06
LEARNING_RATE = 0.02
DECAY_RATE = 0.1
CORES = 2


def widen_kernel(steps, own, place, *refs):
    grads = refs[:steps]
    if own:
        other, outs = refs[steps], refs[steps + 1 :]
        for out in range(2 * steps):
            step, half = divmod(out, 2)
            outs[out][...] = grads[step][0, :, half].astype(jnp.float32) + other[step, half]
    else:
        for step in range(steps):
            for half in range(2):
                refs[-1][step, half] = grads[step][0, :, half].astype(jnp.float32)


def widen(grads, place, size, steps, other=None):
    _, groups, _, rows, columns = grads.shape
    width = columns // size
    deep = groups // 2
    own = other is not None

    def source(step):
        def index(j, place):
            matrix = place[1] if own else 1 - place[1]
            return (matrix, j, 0, 0, lax.rem(place[0] + step, size))

        return pl.BlockSpec((1, deep, 2, rows, width), index)

    flat = pl.BlockSpec((deep, rows, width), lambda j, place: (j, 0, 0))
    count = len(steps)
    joined = pl.BlockSpec((count, 2, deep, rows, width), lambda j, place: (0, 0, j, 0, 0))
    shape = (groups, rows, width)
    shapes = [shape] * (2 * count) if own else [(count, 2) + shape]
    return pl.pallas_call(
        functools.partial(widen_kernel, count, own),
        grid_spec=pltpu.PrefetchScalarGridSpec(
            num_scalar_prefetch=1,
            grid=(2,),
            in_specs=[source(step) for step in steps] + ([joined] if own else []),
            out_specs=[flat] * (2 * count) if own else [joined],
        ),
        out_shape=[jax.ShapeDtypeStruct(s, jnp.float32) for s in shapes],
        compiler_params=pltpu.CompilerParams(vmem_limit_bytes=40 * 2**20),
    )(place, *[grads] * count, *([other] if own else []))


def swap(values):
    return lax.ppermute(values, "core", [(0, 1), (1, 0)])


def move(values, size, step):
    return lax.ppermute(values, "x", [(i, (i + step) % size) for i in range(size)])


def after(values, earlier):
    return lax.optimization_barrier((values, earlier))[0]


def reduce_scatter(grads, place, size):
    def total(steps, sent):
        return widen(grads, place, size, steps, swap(sent))

    (sent,) = widen(grads, place, size, (2,))
    (sent_later,) = widen(grads, after(place, sent), size, (1, 3, 0))
    far_first, far_second = total((2,), sent)
    right = move(far_first, size, 1)
    left = move(far_second, size, -1)
    parts = total((1, 3, 0), after(sent_later, far_first))
    next_first, next_second, last_first, last_second, first, second = parts
    right_plain = move(next_second, size, 1)
    left_plain = move(last_first, size, -1)
    right_summed = move(next_first + right, size, 1)
    left_summed = move(last_second + left, size, -1)
    first = first + left_plain
    second = second + right_plain
    return first + right_summed, second + left_summed


def group_sum(part, axes, size):
    spread = jnp.broadcast_to(part[None, None, :], (size, 1) + part.shape)
    return jnp.sum(lax.all_to_all(spread, axes, 0, 0, tiled=True), axis=(0, 1))


def update_kernel(pieces, weights, updated, direction):
    values = pieces[:, 0]
    direction[...] = values
    updated[...] = weights[...] * (1.0 - LEARNING_RATE * DECAY_RATE) - LEARNING_RATE * values


def update(pieces, weights):
    _, size, rows, width = pieces.shape
    side = pl.BlockSpec((CORES, rows, width), lambda i: (0, 0, i))
    return pl.pallas_call(
        update_kernel,
        grid=(size,),
        in_specs=[pl.BlockSpec((CORES, 1, rows, width), lambda i: (0, i, 0, 0)), side],
        out_specs=[side, side],
        out_shape=[jax.ShapeDtypeStruct(weights.shape, jnp.float32)] * 2,
        compiler_params=pltpu.CompilerParams(vmem_limit_bytes=40 * 2**20),
    )(pieces, weights)


def per_device(sizes, grad_parts, weights):
    size_x, size_row, size_col = sizes
    _, _, blocks, rows, columns = grad_parts.shape
    x = lax.axis_index("x")
    core = lax.axis_index("core")
    place = jnp.stack([x, core]).astype(jnp.int32)
    grads = grad_parts.reshape(2, size_x, CORES, rows, columns)
    halves = reduce_scatter(grads, place, size_x)
    width = columns // size_x

    halves = lax.optimization_barrier(halves)
    values = [jnp.concatenate(halves).reshape(blocks * rows, width)]
    row_factor = jnp.ones((1, blocks * rows), jnp.float32)
    column_factor = jnp.ones((width,), jnp.float32)

    def scaled():
        return [
            v * r[:, None] * column_factor[None, :] for v, r in zip(values, row_factor)
        ]

    for sweep in range(ITERS):
        part = jnp.concatenate([jnp.sum(v * v, axis=1) for v in scaled()])
        total = group_sum(part, ("x", "col"), size_x * size_col)
        row_factor = row_factor * lax.rsqrt(total / FW + EPSILON).reshape(1, -1)
        part = sum(jnp.sum(v * v, axis=0) for v in scaled())
        total = group_sum(part, ("row",), size_row)
        column_factor = column_factor * lax.rsqrt(total / DW + EPSILON)

    direction = scaled()[0].reshape(blocks, rows, width)
    direction = lax.all_to_all(direction, ("core", "x"), 0, 0, tiled=True)
    direction = direction.reshape(CORES, size_x, rows, width)
    return update(direction, weights)


def solution(mesh):
    size_x = mesh.shape["rep"] // CORES
    sizes = (size_x, mesh.shape["row"], mesh.shape["col"])
    split = Mesh(
        mesh.devices.reshape((size_x, CORES) + sizes[1:]), ("x", "core", "row", "col")
    )
    rep = ("x", "core")
    in_specs = (P(rep, None, None, "row", "col"), P(None, rep + ("row",), "col"))
    out_specs = (P(None, rep + ("row",), "col"), P(None, rep + ("row",), "col"))

    def run(grad_parts, weights):
        return per_device(sizes, grad_parts, weights)

    return jax.shard_map(
        run, mesh=split, in_specs=in_specs, out_specs=out_specs, check_vma=False
    )
```
